32 devices in a mesh: groups: 2 (over y), tm: 4 (over z), chan: 2 (over x), dp: 2 (over core).
Axes of the slice: x: 2, y: 2, z: 4, core: 2. Of those that a mesh axis runs over, the one named last changes fastest.
Arguments:
- frames: bfloat16 [4, 32, 16, 16, 512], P(('groups', 'dp'), 'tm'), parts along dimension 0, may hold values from -6 to 6
- w_in: bfloat16 [3, 3, 512, 256], P(None, None, None, 'chan'), may hold values from -0.09375 to 0.09375
- w_out: bfloat16 [3, 3, 256, 512], P(None, None, None, 'chan'), may hold values from -0.01171875 to 0.01171875
- skip: float32 [512], P('chan'), may hold values from -4 to 4
- rates: float32 [256], replicated, may hold values from 0.002 to 0.3, as said below
- steps_dt: float32 [4, 32], P(('groups', 'dp'), 'tm'), parts along dimension 0, may hold values from 0.5 to 80, as said below
Outputs:
- mixed: bfloat16 [4, 32, 16, 16, 512], P(('groups', 'dp'), 'tm', None, None, 'chan'), parts along dimension 0
The draws below stay inside these ranges and needn't reach their ends.
There are 2 independent parts, one for each index of `groups`. The reference program is written for one: setup_inputs(seed, part) draws one part's arguments, and reference() takes and returns one part's arrays. A program takes and returns all parts, laid end to end along the dimension named above; an argument that names none is the same for every part. Nothing has to cross between parts.
Inputs may be any that keep to these rules, and one draw needn't show every extreme that they name: rates are positive. `steps_dt`: time steps are positive.
All inputs are finite; a program needn't handle non-finite values.
Results may differ from the reference program's by a relative error of at most 0.0051.
Values may be sent and summed in bfloat16 or wider, within the bound.
A program may use at most 64 MiB of HBM per device.

```python
import math
import jax
import jax.numpy as jnp
from jax import lax

H = 16
W = 16
U = 512
P_SIZE = 256
CLIP_COUNT = 2
CLIP_IMAGES = 32


def draw_rates(key, part):
    first = jax.random.fold_in(jax.random.fold_in(key, 11), 0)
    return jnp.exp(jax.random.uniform(first, (P_SIZE,), jnp.float32, math.log(0.002), math.log(0.3)))


def draw_steps_dt(key, part):
    first, second, tertiary_argument = jax.random.split(jax.random.fold_in(key, 23), 3)
    starting_index = jax.random.uniform(first, (CLIP_COUNT, CLIP_IMAGES), jnp.float32, 0.5, 1.5)
    places = jax.random.randint(second, (CLIP_COUNT, 3), 0, CLIP_IMAGES)
    marked_lines = jnp.any(jnp.arange(CLIP_IMAGES)[None, None, :] == places[:, :, None], axis=1)
    span_count = jax.random.uniform(tertiary_argument, (CLIP_COUNT, CLIP_IMAGES), jnp.float32, 40.0, 80.0)
    return jnp.where(marked_lines, span_count, starting_index)


def level_of(own_key, extent, cuts, least, high):
    loudness, own = 1.0, jax.random.fold_in(own_key, 6)
    for axis_at, parts in cuts:
        steps = jnp.exp(jax.random.uniform(jax.random.fold_in(own, axis_at), (parts,), jnp.float32, least / len(cuts), high / len(cuts)))
        loudness = loudness * jnp.repeat(steps, extent[axis_at] // parts).reshape([-1 if axis == axis_at else 1 for axis in range(len(extent))])
    return loudness


def centred(stream_key, extent, spread, reach, shards=(), held_as=jnp.bfloat16):
    drawn = jax.random.normal(stream_key, extent, jnp.float32) * spread
    if len(shards) > 0:
        drawn = level_of(stream_key, extent, shards, -0.22, 0.18) * drawn
    return jnp.clip(drawn, min=-reach, max=reach).astype(held_as)


def setup_inputs(seed: int = 0, part: int = 0) -> dict:
    arg_keys = jax.random.split(jax.random.key(seed), 7)
    own_keys = jax.random.split(jax.random.fold_in(arg_keys[6], part), 7)
    return {
        "frames": centred(own_keys[0], (CLIP_COUNT, CLIP_IMAGES, H, W, U), 1.0, 6.0, ((0, 2), (1, 4))),
        "w_in": centred(arg_keys[1], (3, 3, U, P_SIZE), (9 * U) ** -0.5, 0.09375, ((3, 2),)),
        "w_out": centred(arg_keys[2], (3, 3, P_SIZE, U), (900 * P_SIZE) ** -0.5, 0.01171875, ((3, 2),)),
        "skip": centred(arg_keys[3], (U,), 1.0, 4.0, ((0, 2),), jnp.float32),
        "rates": draw_rates(jax.random.fold_in(arg_keys[6], 71), part),
        "steps_dt": draw_steps_dt(jax.random.fold_in(jax.random.fold_in(arg_keys[6], part), 71), part),
    }


def conv_three(values, weight):
    height = values.shape[2]
    width = values.shape[3]
    channels = values.shape[4]
    padded = jnp.pad(values, ((0, 0), (0, 0), (1, 1), (1, 1), (0, 0)))
    total = jnp.zeros(values.shape[:4] + (weight.shape[3],), jnp.float32)
    for row_off in range(3):
        for col_off in range(3):
            window = padded[:, :, row_off:row_off + height, col_off:col_off + width, :].reshape(-1, channels)
            term = jnp.dot(window, weight[row_off, col_off], precision=lax.Precision.HIGHEST)
            total = total + term.reshape(total.shape)
    return total


def reference(frames, w_in, w_out, skip, rates, steps_dt):
    frames_wide = frames.astype(jnp.float32)
    drive = conv_three(frames_wide, w_in.astype(jnp.float32))
    scaled = rates[None, None, :] * steps_dt[:, :, None]
    decay = jnp.exp(-scaled)
    gain_in = -jnp.expm1(-scaled) / rates[None, None, :]

    def advance(state, inputs):
        dec, gin, push = inputs
        state = dec[:, None, None, :] * state + gin[:, None, None, :] * push
        return state, state

    start = jnp.zeros((drive.shape[0], drive.shape[2], drive.shape[3], drive.shape[4]), jnp.float32)
    _, history = lax.scan(advance, start, (jnp.moveaxis(decay, 1, 0), jnp.moveaxis(gain_in, 1, 0), jnp.moveaxis(drive, 1, 0)))
    states = jnp.moveaxis(history, 0, 1).astype(jnp.bfloat16)
    mixed = conv_three(states.astype(jnp.float32), w_out.astype(jnp.float32)) + skip * frames_wide
    return mixed.astype(jnp.bfloat16)
```

```python
import functools

import jax
import jax.numpy as jnp
from jax import lax
from jax.experimental import pallas as pl
from jax.experimental.pallas import tpu as pltpu
from jax.sharding import PartitionSpec as P


def from_behind(block, axis, distance):
    devices = range(lax.axis_size(axis))
    route = [(i - distance, i) for i in devices if i - distance in devices]
    return lax.ppermute(block, axis, route)


def pad_grid(values):
    return jnp.pad(values, ((0, 0), (0, 0), (1, 1), (1, 1), (0, 0)))


def displaced_filter(padded, weight, total):
    height = padded.shape[2] - 2
    width = padded.shape[3] - 2
    channels = padded.shape[4]
    for row_off in range(3):
        for col_off in range(3):
            window = padded[:, :, row_off : row_off + height, col_off : col_off + width, :].reshape(
                -1, channels
            )
            term = jnp.dot(window, weight[row_off, col_off], preferred_element_type=jnp.float32)
            total = total + term.reshape(total.shape)
    return total


def combine_operator(earlier, later):
    return (earlier[0] * later[0], later[0] * earlier[1] + later[1])


def block_states(frames, weight_in, rate_part, steps_dt):
    batch_n, frame_n, height, width = frames.shape[:4]
    chans = weight_in.shape[3]
    shape_out = frames.shape[:4] + (chans,)
    drive = displaced_filter(pad_grid(frames), weight_in, jnp.zeros(shape_out, jnp.float32))
    flat_drive = drive.reshape(batch_n, frame_n, height, width * chans)
    scaled = rate_part[None, None, :] * steps_dt[:, :, None]
    decay = jnp.exp(-scaled)
    gain_in = -jnp.expm1(-scaled) / rate_part[None, None, :]
    decay_flat = jnp.tile(decay, (1, 1, width))[:, :, None, :]
    gain_flat = jnp.tile(gain_in, (1, 1, width))[:, :, None, :]
    running_product, local_state = lax.associative_scan(
        combine_operator, (decay_flat, gain_flat * flat_drive), axis=1
    )
    total_decay = running_product[:, -1]
    end_state = local_state[:, -1]

    def relay(index, incoming):
        return from_behind(total_decay * incoming + end_state, "tm", 1)

    carried = lax.fori_loop(0, lax.axis_size("tm") - 1, relay, jnp.zeros_like(end_state))
    full_state = local_state + running_product * carried[:, None]
    return full_state.astype(jnp.bfloat16)


def on_device(frames, w_in, w_out, skip, rates, steps_dt):
    feat_part = w_out.shape[3]
    state_part = w_in.shape[3]
    batch_n, frame_n, height, width = frames.shape[:4]
    own_chan = lax.axis_index("chan")
    out_shape = frames.shape[:4] + (feat_part,)
    rate_part = lax.dynamic_slice_in_dim(rates, own_chan * state_part, state_part, 0)
    flat_states = block_states(frames, w_in, rate_part, steps_dt)
    block_width = width * state_part
    piece = lax.all_gather(flat_states, "chan", axis=3, tiled=True)
    partitions = piece.shape[3] // block_width
    grid = piece.reshape(batch_n, frame_n, height, partitions, width, state_part)
    grid = jnp.moveaxis(grid, 3, 4).reshape(
        batch_n, frame_n, height, width, partitions * state_part
    )
    outcome = displaced_filter(pad_grid(grid), w_out, jnp.zeros(out_shape, jnp.float32))
    own_feats = lax.dynamic_slice_in_dim(frames, own_chan * feat_part, feat_part, 4)
    mixed = outcome + skip * own_feats.astype(jnp.float32)
    return mixed.astype(jnp.bfloat16)


LANES = 128
MESH = pl.DeviceIdType.MESH


def fused_kernel(
    dims,
    frames_hbm,
    w_in_hbm,
    w_out_hbm,
    skip_ref,
    rates_ref,
    steps_ref,
    out_hbm,
    frames_buf,
    w_in_buf,
    w_out_buf,
    out_buf,
    states,
    running,
    ends,
    block_decay,
    carry,
    taps,
    frame_sem,
    w_in_sem,
    w_out_sem,
    out_sem,
    state_send,
    state_recv,
    end_send,
    end_recv,
    decay_send,
    decay_recv,
    carry_send,
    carry_recv,
):
    blocks, count, height, width, group = dims
    cells = height * width
    rows = group * cells
    groups_n = count // group
    part = running.shape[1]
    feats = out_buf.shape[1]
    chans = 2 * part
    me = lax.axis_index("chan")
    other = 1 - me
    z = lax.axis_index("tm")

    def frame_copy(g):
        span = pl.ds(pl.multiple_of(g * rows, rows), rows)
        return pltpu.make_async_copy(
            frames_hbm.at[span], frames_buf.at[span], frame_sem.at[g]
        )

    def w_in_copy(tap):
        row_off, col_off = tap // 3, tap % 3
        place = (col_off * 3 + row_off) * part
        return pltpu.make_async_copy(
            w_in_hbm.at[tap], w_in_buf.at[:, place : place + part], w_in_sem.at[tap]
        )

    def out_copy(g):
        span = pl.ds(pl.multiple_of(g * rows, rows), rows)
        return pltpu.make_async_copy(out_buf.at[span], out_hbm.at[span], out_sem.at[g])

    w_out_copy = pltpu.make_async_copy(w_out_hbm, w_out_buf, w_out_sem)
    for tap in range(9):
        w_in_copy(tap).start()
    for g in range(groups_n):
        frame_copy(g).start()
    w_out_copy.start()

    barrier = pltpu.get_barrier_semaphore()
    pl.semaphore_signal(barrier, inc=1, device_id={"chan": other}, device_id_type=MESH)
    for k in range(blocks):

        @pl.when(k != z)
        def _():
            pl.semaphore_signal(barrier, inc=1, device_id={"tm": k}, device_id_type=MESH)

    rates_all = rates_ref[...]
    rates_own = rates_ref[:, pl.ds(pl.multiple_of(me * part, part), part)]
    total = steps_ref[0, 0]
    for t in range(1, count):
        total = total + steps_ref[0, t]
    block_decay[z] = jnp.broadcast_to(jnp.exp(-rates_own * total), (8, part))
    running[...] = jnp.zeros_like(running)
    taps[...] = jnp.zeros_like(taps)
    pl.semaphore_wait(barrier, blocks)

    def decay_send_to(k):
        return pltpu.make_async_remote_copy(
            src_ref=block_decay.at[z],
            dst_ref=block_decay.at[z],
            send_sem=decay_send.at[k],
            recv_sem=decay_recv.at[z],
            device_id={"tm": k},
            device_id_type=MESH,
        )

    def decay_from(k):
        return pltpu.make_async_remote_copy(
            src_ref=block_decay.at[k],
            dst_ref=block_decay.at[k],
            send_sem=decay_send.at[k],
            recv_sem=decay_recv.at[k],
            device_id={"tm": k},
            device_id_type=MESH,
        )

    def end_send_to(k):
        return pltpu.make_async_remote_copy(
            src_ref=states.at[me, count - 1],
            dst_ref=ends.at[z],
            send_sem=end_send.at[k],
            recv_sem=end_recv.at[z],
            device_id={"tm": k},
            device_id_type=MESH,
        )

    def end_from(k):
        return pltpu.make_async_remote_copy(
            src_ref=states.at[me, count - 1],
            dst_ref=ends.at[k],
            send_sem=end_send.at[k],
            recv_sem=end_recv.at[k],
            device_id={"tm": k},
            device_id_type=MESH,
        )

    def state_copy(side, t):
        return pltpu.make_async_remote_copy(
            src_ref=states.at[side, t],
            dst_ref=states.at[side, t],
            send_sem=state_send.at[t],
            recv_sem=state_recv.at[t],
            device_id={"chan": other},
            device_id_type=MESH,
        )

    def carry_copy(side):
        return pltpu.make_async_remote_copy(
            src_ref=carry.at[side],
            dst_ref=carry.at[side],
            send_sem=carry_send,
            recv_sem=carry_recv,
            device_id={"chan": other},
            device_id_type=MESH,
        )

    for k in range(1, blocks):

        @pl.when(z < k)
        def _():
            decay_send_to(k).start()

    for tap in range(9):
        w_in_copy(tap).wait()

    column = lax.broadcasted_iota(jnp.int32, (cells, 1), 0) % width
    first_col = column == 0
    last_col = column == width - 1

    def drive_step(g, unused):
        frame_copy(g).wait()
        span = pl.ds(pl.multiple_of(g * rows, rows), rows)
        product = jnp.dot(
            frames_buf[span, :], w_in_buf[...], preferred_element_type=jnp.float32
        )
        for f in range(group):
            t = g * group + f
            mine = product[f * cells : (f + 1) * cells]
            sums = []
            for col_off in range(3):
                base = col_off * 3 * part
                above = mine[:, base : base + part]
                level = mine[:, base + part : base + 2 * part]
                below = mine[:, base + 2 * part : base + 3 * part]
                zero = jnp.zeros((width, part), jnp.float32)
                sums.append(
                    level
                    + jnp.concatenate([zero, above[: cells - width]], axis=0)
                    + jnp.concatenate([below[width:], zero], axis=0)
                )
            drive = (
                sums[1]
                + jnp.where(first_col, 0.0, pltpu.roll(sums[0], 1, 0))
                + jnp.where(last_col, 0.0, pltpu.roll(sums[2], cells - 1, 0))
            )
            scaled = rates_own * steps_ref[0, t]
            decay = jnp.exp(-scaled)
            gain_in = (1.0 - decay) / rates_own
            state = decay * running[...] + gain_in * drive
            running[...] = state
            states[me, t] = state.astype(jnp.bfloat16)
            state_copy(me, t).start()
        return unused

    lax.fori_loop(0, groups_n, drive_step, 0)

    for k in reversed(range(1, blocks)):

        @pl.when(z < k)
        def _():
            end_send_to(k).start()

    running[...] = jnp.zeros_like(running)
    for k in range(blocks - 1):

        @pl.when(k < z)
        def _():
            decay_from(k).wait_recv()
            end_from(k).wait_recv()
            running[...] = block_decay[k][:1] * running[...] + ends[k].astype(jnp.float32)

    carry[me] = running[...].astype(jnp.bfloat16)
    carry_copy(me).start()
    w_out_copy.wait()
    carry_copy(other).wait_recv()

    own_feats = pl.ds(pl.multiple_of(me * feats, feats), feats)

    def mix_step(g, elapsed):
        span = pl.ds(pl.multiple_of(g * rows, rows), rows)
        for f in range(group):
            t = g * group + f
            state_copy(other, t).wait_recv()
            elapsed = elapsed + steps_ref[0, t]
            product = jnp.exp(-rates_all * elapsed)
            for side in range(2):
                lanes = slice(side * part, (side + 1) * part)
                state = states[side, t].astype(jnp.float32) + product[:, lanes] * carry[
                    side
                ].astype(jnp.float32)
                state = state.astype(jnp.bfloat16).astype(jnp.float32)
                held = (
                    jnp.where(first_col, 0.0, pltpu.roll(state, 1, 0)),
                    state,
                    jnp.where(last_col, 0.0, pltpu.roll(state, cells - 1, 0)),
                )
                for col_off in range(3):
                    at = col_off * chans + side * part
                    taps[f, width : width + cells, at : at + part] = held[col_off].astype(
                        jnp.bfloat16
                    )
        result = None
        for row_off in range(3):
            window = taps[:, row_off * width : row_off * width + cells, :].reshape(rows, 3 * chans)
            term = jnp.dot(
                window,
                w_out_buf[row_off * 3 * chans : (row_off + 1) * 3 * chans, :],
                preferred_element_type=jnp.float32,
            )
            result = term if result is None else result + term
        result = result + skip_ref[...] * frames_buf[span, own_feats].astype(jnp.float32)
        out_buf[span, :] = result.astype(jnp.bfloat16)
        out_copy(g).start()
        return elapsed

    lax.fori_loop(0, groups_n, mix_step, jnp.float32(0.0))

    for g in range(groups_n):
        out_copy(g).wait()
    for t in range(count):
        state_copy(me, t).wait_send()
    carry_copy(me).wait_send()
    for k in range(1, blocks):

        @pl.when(z < k)
        def _():
            decay_send_to(k).wait_send()
            end_send_to(k).wait_send()


def on_device_fused(frames, w_in, w_out, skip, rates, steps_dt):
    _, count, height, width, feats_in = frames.shape
    part, feats = w_in.shape[3], w_out.shape[3]
    chans = w_out.shape[2]
    blocks = lax.axis_size("tm")
    cells = height * width
    group = 2
    groups_n = count // group
    dims = (blocks, count, height, width, group)
    hbm = pl.BlockSpec(memory_space=pltpu.HBM)
    vmem = pl.BlockSpec(memory_space=pltpu.VMEM)
    smem = pl.BlockSpec(memory_space=pltpu.SMEM)
    dma = pltpu.SemaphoreType.DMA
    out = pl.pallas_call(
        functools.partial(fused_kernel, dims),
        out_shape=jax.ShapeDtypeStruct((count * cells, feats), jnp.bfloat16),
        in_specs=[hbm, hbm, hbm, vmem, vmem, smem],
        out_specs=pl.BlockSpec(memory_space=pl.ANY),
        scratch_shapes=[
            pltpu.VMEM((count * cells, feats_in), jnp.bfloat16),
            pltpu.VMEM((feats_in, 9 * part), jnp.bfloat16),
            pltpu.VMEM((9 * chans, feats), jnp.bfloat16),
            pltpu.VMEM((count * cells, feats), jnp.bfloat16),
            pltpu.VMEM((2, count, cells, part), jnp.bfloat16),
            pltpu.VMEM((cells, part), jnp.float32),
            pltpu.VMEM((blocks, cells, part), jnp.bfloat16),
            pltpu.VMEM((blocks, 8, part), jnp.float32),
            pltpu.VMEM((2, cells, part), jnp.bfloat16),
            pltpu.VMEM((group, cells + 2 * width, 3 * chans), jnp.bfloat16),
            dma((groups_n,)),
            dma((9,)),
            dma,
            dma((groups_n,)),
            dma((count,)),
            dma((count,)),
            dma((blocks,)),
            dma((blocks,)),
            dma((blocks,)),
            dma((blocks,)),
            dma,
            dma,
        ],
        compiler_params=pltpu.CompilerParams(
            collective_id=0, has_side_effects=True, vmem_limit_bytes=48 << 20
        ),
    )(
        frames.reshape(count * cells, feats_in),
        w_in.reshape(9, feats_in, part),
        w_out.reshape(9 * chans, feats),
        skip.reshape(1, feats),
        rates.reshape(1, chans),
        steps_dt,
    )
    return out.reshape(1, count, height, width, feats)


def pick(mesh, frames, w_in, w_out, skip, rates, steps_dt):
    clips, count, height, width = frames.shape[:4]
    fused = (
        mesh.shape["chan"] == 2
        and clips == 1
        and count % 2 == 0
        and width == 16
        and w_in.shape[3] == LANES
        and w_out.shape[3] % LANES == 0
    )
    body = on_device_fused if fused else on_device
    return body(frames, w_in, w_out, skip, rates, steps_dt)


def solution(mesh):
    return jax.shard_map(
        functools.partial(pick, mesh),
        mesh=mesh,
        in_specs=(
            P(("groups", "dp"), "tm", None, None, None),
            P(None, None, None, "chan"),
            P(None, None, None, "chan"),
            P("chan"),
            P(),
            P(("groups", "dp"), "tm"),
        ),
        out_specs=P(("groups", "dp"), "tm", None, None, "chan"),
        check_vma=False,
    )
```

```python
import functools

import jax
import jax.numpy as jnp
from jax import lax
from jax.experimental import pallas as pl
from jax.experimental.pallas import tpu as pltpu
from jax.sharding import PartitionSpec as P


def from_behind(block, axis, distance):
    devices = range(lax.axis_size(axis))
    route = [(i - distance, i) for i in devices if i - distance in devices]
    return lax.ppermute(block, axis, route)


def pad_grid(values):
    return jnp.pad(values, ((0, 0), (0, 0), (1, 1), (1, 1), (0, 0)))


def displaced_filter(padded, weight, total):
    height = padded.shape[2] - 2
    width = padded.shape[3] - 2
    channels = padded.shape[4]
    for row_off in range(3):
        for col_off in range(3):
            window = padded[:, :, row_off : row_off + height, col_off : col_off + width, :].reshape(
                -1, channels
            )
            term = jnp.dot(window, weight[row_off, col_off], preferred_element_type=jnp.float32)
            total = total + term.reshape(total.shape)
    return total


def combine_operator(earlier, later):
    return (earlier[0] * later[0], later[0] * earlier[1] + later[1])


def block_states(frames, weight_in, rate_part, steps_dt):
    batch_n, frame_n, height, width = frames.shape[:4]
    chans = weight_in.shape[3]
    shape_out = frames.shape[:4] + (chans,)
    drive = displaced_filter(pad_grid(frames), weight_in, jnp.zeros(shape_out, jnp.float32))
    flat_drive = drive.reshape(batch_n, frame_n, height, width * chans)
    scaled = rate_part[None, None, :] * steps_dt[:, :, None]
    decay = jnp.exp(-scaled)
    gain_in = -jnp.expm1(-scaled) / rate_part[None, None, :]
    decay_flat = jnp.tile(decay, (1, 1, width))[:, :, None, :]
    gain_flat = jnp.tile(gain_in, (1, 1, width))[:, :, None, :]
    running_product, local_state = lax.associative_scan(
        combine_operator, (decay_flat, gain_flat * flat_drive), axis=1
    )
    total_decay = running_product[:, -1]
    end_state = local_state[:, -1]

    def relay(index, incoming):
        return from_behind(total_decay * incoming + end_state, "tm", 1)

    carried = lax.fori_loop(0, lax.axis_size("tm") - 1, relay, jnp.zeros_like(end_state))
    full_state = local_state + running_product * carried[:, None]
    return full_state.astype(jnp.bfloat16)


def on_device(frames, w_in, w_out, skip, rates, steps_dt):
    feat_part = w_out.shape[3]
    state_part = w_in.shape[3]
    batch_n, frame_n, height, width = frames.shape[:4]
    own_chan = lax.axis_index("chan")
    out_shape = frames.shape[:4] + (feat_part,)
    rate_part = lax.dynamic_slice_in_dim(rates, own_chan * state_part, state_part, 0)
    flat_states = block_states(frames, w_in, rate_part, steps_dt)
    block_width = width * state_part
    piece = lax.all_gather(flat_states, "chan", axis=3, tiled=True)
    partitions = piece.shape[3] // block_width
    grid = piece.reshape(batch_n, frame_n, height, partitions, width, state_part)
    grid = jnp.moveaxis(grid, 3, 4).reshape(
        batch_n, frame_n, height, width, partitions * state_part
    )
    outcome = displaced_filter(pad_grid(grid), w_out, jnp.zeros(out_shape, jnp.float32))
    own_feats = lax.dynamic_slice_in_dim(frames, own_chan * feat_part, feat_part, 4)
    mixed = outcome + skip * own_feats.astype(jnp.float32)
    return mixed.astype(jnp.bfloat16)


LANES = 128
MESH = pl.DeviceIdType.MESH


def fused_kernel(
    dims,
    frames_hbm,
    w_in_hbm,
    w_out_hbm,
    skip_hbm,
    rates_hbm,
    steps_hbm,
    out_hbm,
    skip_ref,
    rates_ref,
    steps_ref,
    frames_buf,
    w_in_buf,
    w_out_buf,
    out_buf,
    states,
    running,
    ends,
    block_decay,
    carry,
    taps,
    frame_sem,
    w_in_sem,
    w_out_sem,
    out_sem,
    state_send,
    state_recv,
    end_send,
    end_recv,
    decay_send,
    decay_recv,
    carry_send,
    carry_recv,
    small_sem,
):
    blocks, count, height, width, group = dims
    cells = height * width
    rows = group * cells
    groups_n = count // group
    part = running.shape[1]
    feats = out_buf.shape[1]
    chans = 2 * part
    me = lax.axis_index("chan")
    other = 1 - me
    z = lax.axis_index("tm")

    def frame_copy(g):
        span = pl.ds(pl.multiple_of(g * rows, rows), rows)
        return pltpu.make_async_copy(
            frames_hbm.at[span], frames_buf.at[span], frame_sem.at[g]
        )

    def w_in_copy(tap):
        row_off, col_off = tap // 3, tap % 3
        place = (col_off * 3 + row_off) * part
        return pltpu.make_async_copy(
            w_in_hbm.at[tap], w_in_buf.at[:, place : place + part], w_in_sem.at[tap]
        )

    def out_copy(g):
        span = pl.ds(pl.multiple_of(g * rows, rows), rows)
        return pltpu.make_async_copy(out_buf.at[span], out_hbm.at[span], out_sem.at[g])

    w_out_copy = pltpu.make_async_copy(w_out_hbm, w_out_buf, w_out_sem)
    small = [
        pltpu.make_async_copy(steps_hbm, steps_ref, small_sem.at[0]),
        pltpu.make_async_copy(rates_hbm, rates_ref, small_sem.at[1]),
        pltpu.make_async_copy(skip_hbm, skip_ref, small_sem.at[2]),
    ]
    for copy in small:
        copy.start()
    for tap in range(9):
        w_in_copy(tap).start()
    for g in range(groups_n):
        frame_copy(g).start()
    w_out_copy.start()

    barrier = pltpu.get_barrier_semaphore()
    pl.semaphore_signal(barrier, inc=1, device_id={"chan": other}, device_id_type=MESH)
    for k in range(blocks):

        @pl.when(k != z)
        def _():
            pl.semaphore_signal(barrier, inc=1, device_id={"tm": k}, device_id_type=MESH)

    for copy in small:
        copy.wait()
    rates_all = rates_ref[...]
    rates_own = rates_ref[:, pl.ds(pl.multiple_of(me * part, part), part)]
    total = steps_ref[0, 0]
    for t in range(1, count):
        total = total + steps_ref[0, t]
    block_decay[z] = jnp.broadcast_to(jnp.exp(-rates_own * total), (8, part))
    running[...] = jnp.zeros_like(running)
    taps[...] = jnp.zeros_like(taps)
    pl.semaphore_wait(barrier, blocks)

    def decay_send_to(k):
        return pltpu.make_async_remote_copy(
            src_ref=block_decay.at[z],
            dst_ref=block_decay.at[z],
            send_sem=decay_send.at[k],
            recv_sem=decay_recv.at[z],
            device_id={"tm": k},
            device_id_type=MESH,
        )

    def decay_from(k):
        return pltpu.make_async_remote_copy(
            src_ref=block_decay.at[k],
            dst_ref=block_decay.at[k],
            send_sem=decay_send.at[k],
            recv_sem=decay_recv.at[k],
            device_id={"tm": k},
            device_id_type=MESH,
        )

    def end_send_to(k):
        return pltpu.make_async_remote_copy(
            src_ref=states.at[me, count - 1],
            dst_ref=ends.at[z],
            send_sem=end_send.at[k],
            recv_sem=end_recv.at[z],
            device_id={"tm": k},
            device_id_type=MESH,
        )

    def end_from(k):
        return pltpu.make_async_remote_copy(
            src_ref=states.at[me, count - 1],
            dst_ref=ends.at[k],
            send_sem=end_send.at[k],
            recv_sem=end_recv.at[k],
            device_id={"tm": k},
            device_id_type=MESH,
        )

    def state_copy(side, t):
        return pltpu.make_async_remote_copy(
            src_ref=states.at[side, t],
            dst_ref=states.at[side, t],
            send_sem=state_send.at[t],
            recv_sem=state_recv.at[t],
            device_id={"chan": other},
            device_id_type=MESH,
        )

    def carry_copy(side):
        return pltpu.make_async_remote_copy(
            src_ref=carry.at[side],
            dst_ref=carry.at[side],
            send_sem=carry_send,
            recv_sem=carry_recv,
            device_id={"chan": other},
            device_id_type=MESH,
        )

    for k in range(1, blocks):

        @pl.when(z < k)
        def _():
            decay_send_to(k).start()

    for tap in range(9):
        w_in_copy(tap).wait()

    column = lax.broadcasted_iota(jnp.int32, (cells, 1), 0) % width
    first_col = column == 0
    last_col = column == width - 1

    def drive_step(g, unused):
        frame_copy(g).wait()
        span = pl.ds(pl.multiple_of(g * rows, rows), rows)
        product = jnp.dot(
            frames_buf[span, :], w_in_buf[...], preferred_element_type=jnp.float32
        )
        for f in range(group):
            t = g * group + f
            mine = product[f * cells : (f + 1) * cells]
            sums = []
            for col_off in range(3):
                base = col_off * 3 * part
                above = mine[:, base : base + part]
                level = mine[:, base + part : base + 2 * part]
                below = mine[:, base + 2 * part : base + 3 * part]
                zero = jnp.zeros((width, part), jnp.float32)
                sums.append(
                    level
                    + jnp.concatenate([zero, above[: cells - width]], axis=0)
                    + jnp.concatenate([below[width:], zero], axis=0)
                )
            drive = (
                sums[1]
                + jnp.where(first_col, 0.0, pltpu.roll(sums[0], 1, 0))
                + jnp.where(last_col, 0.0, pltpu.roll(sums[2], cells - 1, 0))
            )
            scaled = rates_own * steps_ref[0, t]
            decay = jnp.exp(-scaled)
            gain_in = (1.0 - decay) / rates_own
            state = decay * running[...] + gain_in * drive
            running[...] = state
            states[me, t] = state.astype(jnp.bfloat16)
            state_copy(me, t).start()
        return unused

    lax.fori_loop(0, groups_n, drive_step, 0)

    for k in reversed(range(1, blocks)):

        @pl.when(z < k)
        def _():
            end_send_to(k).start()

    running[...] = jnp.zeros_like(running)
    for k in range(blocks - 1):

        @pl.when(k < z)
        def _():
            decay_from(k).wait_recv()
            end_from(k).wait_recv()
            running[...] = block_decay[k][:1] * running[...] + ends[k].astype(jnp.float32)

    carry[me] = running[...].astype(jnp.bfloat16)
    carry_copy(me).start()
    w_out_copy.wait()
    carry_copy(other).wait_recv()

    own_feats = pl.ds(pl.multiple_of(me * feats, feats), feats)

    def mix_step(g, elapsed):
        span = pl.ds(pl.multiple_of(g * rows, rows), rows)
        for f in range(group):
            t = g * group + f
            state_copy(other, t).wait_recv()
            elapsed = elapsed + steps_ref[0, t]
            product = jnp.exp(-rates_all * elapsed)
            for side in range(2):
                lanes = slice(side * part, (side + 1) * part)
                state = states[side, t].astype(jnp.float32) + product[:, lanes] * carry[
                    side
                ].astype(jnp.float32)
                state = state.astype(jnp.bfloat16).astype(jnp.float32)
                held = (
                    jnp.where(first_col, 0.0, pltpu.roll(state, 1, 0)),
                    state,
                    jnp.where(last_col, 0.0, pltpu.roll(state, cells - 1, 0)),
                )
                for col_off in range(3):
                    at = col_off * chans + side * part
                    taps[f, width : width + cells, at : at + part] = held[col_off].astype(
                        jnp.bfloat16
                    )
        result = None
        for row_off in range(3):
            window = taps[:, row_off * width : row_off * width + cells, :].reshape(rows, 3 * chans)
            term = jnp.dot(
                window,
                w_out_buf[row_off * 3 * chans : (row_off + 1) * 3 * chans, :],
                preferred_element_type=jnp.float32,
            )
            result = term if result is None else result + term
        result = result + skip_ref[...] * frames_buf[span, own_feats].astype(jnp.float32)
        out_buf[span, :] = result.astype(jnp.bfloat16)
        out_copy(g).start()
        return elapsed

    lax.fori_loop(0, groups_n, mix_step, jnp.float32(0.0))

    for g in range(groups_n):
        out_copy(g).wait()
    for t in range(count):
        state_copy(me, t).wait_send()
    carry_copy(me).wait_send()
    for k in range(1, blocks):

        @pl.when(z < k)
        def _():
            decay_send_to(k).wait_send()
            end_send_to(k).wait_send()


def on_device_fused(frames, w_in, w_out, skip, rates, steps_dt):
    _, count, height, width, feats_in = frames.shape
    part, feats = w_in.shape[3], w_out.shape[3]
    chans = w_out.shape[2]
    blocks = lax.axis_size("tm")
    cells = height * width
    group = 2
    groups_n = count // group
    dims = (blocks, count, height, width, group)
    hbm = pl.BlockSpec(memory_space=pltpu.HBM)
    dma = pltpu.SemaphoreType.DMA
    out = pl.pallas_call(
        functools.partial(fused_kernel, dims),
        out_shape=jax.ShapeDtypeStruct((count * cells, feats), jnp.bfloat16),
        in_specs=[hbm] * 6,
        out_specs=pl.BlockSpec(memory_space=pl.ANY),
        scratch_shapes=[
            pltpu.VMEM((1, feats), jnp.float32),
            pltpu.VMEM((1, chans), jnp.float32),
            pltpu.SMEM((1, count), jnp.float32),
            pltpu.VMEM((count * cells, feats_in), jnp.bfloat16),
            pltpu.VMEM((feats_in, 9 * part), jnp.bfloat16),
            pltpu.VMEM((9 * chans, feats), jnp.bfloat16),
            pltpu.VMEM((count * cells, feats), jnp.bfloat16),
            pltpu.VMEM((2, count, cells, part), jnp.bfloat16),
            pltpu.VMEM((cells, part), jnp.float32),
            pltpu.VMEM((blocks, cells, part), jnp.bfloat16),
            pltpu.VMEM((blocks, 8, part), jnp.float32),
            pltpu.VMEM((2, cells, part), jnp.bfloat16),
            pltpu.VMEM((group, cells + 2 * width, 3 * chans), jnp.bfloat16),
            dma((groups_n,)),
            dma((9,)),
            dma,
            dma((groups_n,)),
            dma((count,)),
            dma((count,)),
            dma((blocks,)),
            dma((blocks,)),
            dma((blocks,)),
            dma((blocks,)),
            dma,
            dma,
            dma((3,)),
        ],
        compiler_params=pltpu.CompilerParams(
            collective_id=0, has_side_effects=True, vmem_limit_bytes=62 << 20
        ),
    )(
        frames.reshape(count * cells, feats_in),
        w_in.reshape(9, feats_in, part),
        w_out.reshape(9 * chans, feats),
        skip.reshape(1, feats),
        rates.reshape(1, chans),
        steps_dt,
    )
    return out.reshape(1, count, height, width, feats)


def pick(mesh, frames, w_in, w_out, skip, rates, steps_dt):
    clips, count, height, width = frames.shape[:4]
    fused = (
        mesh.shape["chan"] == 2
        and clips == 1
        and count % 2 == 0
        and width == 16
        and w_in.shape[3] == LANES
        and w_out.shape[3] % LANES == 0
    )
    body = on_device_fused if fused else on_device
    return body(frames, w_in, w_out, skip, rates, steps_dt)


def solution(mesh):
    return jax.shard_map(
        functools.partial(pick, mesh),
        mesh=mesh,
        in_specs=(
            P(("groups", "dp"), "tm", None, None, None),
            P(None, None, None, "chan"),
            P(None, None, None, "chan"),
            P("chan"),
            P(),
            P(("groups", "dp"), "tm"),
        ),
        out_specs=P(("groups", "dp"), "tm", None, None, "chan"),
        check_vma=False,
    )
```

```python
import functools

import jax
import jax.numpy as jnp
from jax import lax
from jax.experimental import pallas as pl
from jax.experimental.pallas import tpu as pltpu
from jax.sharding import PartitionSpec as P


def from_behind(block, axis, distance):
    devices = range(lax.axis_size(axis))
    route = [(i - distance, i) for i in devices if i - distance in devices]
    return lax.ppermute(block, axis, route)


def pad_grid(values):
    return jnp.pad(values, ((0, 0), (0, 0), (1, 1), (1, 1), (0, 0)))


def displaced_filter(padded, weight, total):
    height = padded.shape[2] - 2
    width = padded.shape[3] - 2
    channels = padded.shape[4]
    for row_off in range(3):
        for col_off in range(3):
            window = padded[:, :, row_off : row_off + height, col_off : col_off + width, :].reshape(
                -1, channels
            )
            term = jnp.dot(window, weight[row_off, col_off], preferred_element_type=jnp.float32)
            total = total + term.reshape(total.shape)
    return total


def combine_operator(earlier, later):
    return (earlier[0] * later[0], later[0] * earlier[1] + later[1])


def block_states(frames, weight_in, rate_part, steps_dt):
    batch_n, frame_n, height, width = frames.shape[:4]
    chans = weight_in.shape[3]
    shape_out = frames.shape[:4] + (chans,)
    drive = displaced_filter(pad_grid(frames), weight_in, jnp.zeros(shape_out, jnp.float32))
    flat_drive = drive.reshape(batch_n, frame_n, height, width * chans)
    scaled = rate_part[None, None, :] * steps_dt[:, :, None]
    decay = jnp.exp(-scaled)
    gain_in = -jnp.expm1(-scaled) / rate_part[None, None, :]
    decay_flat = jnp.tile(decay, (1, 1, width))[:, :, None, :]
    gain_flat = jnp.tile(gain_in, (1, 1, width))[:, :, None, :]
    running_product, local_state = lax.associative_scan(
        combine_operator, (decay_flat, gain_flat * flat_drive), axis=1
    )
    total_decay = running_product[:, -1]
    end_state = local_state[:, -1]

    def relay(index, incoming):
        return from_behind(total_decay * incoming + end_state, "tm", 1)

    carried = lax.fori_loop(0, lax.axis_size("tm") - 1, relay, jnp.zeros_like(end_state))
    full_state = local_state + running_product * carried[:, None]
    return full_state.astype(jnp.bfloat16)


def on_device(frames, w_in, w_out, skip, rates, steps_dt):
    feat_part = w_out.shape[3]
    state_part = w_in.shape[3]
    batch_n, frame_n, height, width = frames.shape[:4]
    own_chan = lax.axis_index("chan")
    out_shape = frames.shape[:4] + (feat_part,)
    rate_part = lax.dynamic_slice_in_dim(rates, own_chan * state_part, state_part, 0)
    flat_states = block_states(frames, w_in, rate_part, steps_dt)
    block_width = width * state_part
    piece = lax.all_gather(flat_states, "chan", axis=3, tiled=True)
    partitions = piece.shape[3] // block_width
    grid = piece.reshape(batch_n, frame_n, height, partitions, width, state_part)
    grid = jnp.moveaxis(grid, 3, 4).reshape(
        batch_n, frame_n, height, width, partitions * state_part
    )
    outcome = displaced_filter(pad_grid(grid), w_out, jnp.zeros(out_shape, jnp.float32))
    own_feats = lax.dynamic_slice_in_dim(frames, own_chan * feat_part, feat_part, 4)
    mixed = outcome + skip * own_feats.astype(jnp.float32)
    return mixed.astype(jnp.bfloat16)


LANES = 128
MESH = pl.DeviceIdType.MESH


def fused_kernel(
    dims,
    frames_hbm,
    w_in_hbm,
    w_out_hbm,
    skip_hbm,
    rates_hbm,
    steps_hbm,
    out_ref,
    skip_ref,
    rates_ref,
    steps_ref,
    frames_buf,
    w_in_buf,
    w_far_buf,
    w_out_buf,
    states,
    running,
    far_drive,
    ends,
    block_decay,
    carry,
    taps,
    frame_sem,
    w_in_sem,
    w_out_sem,
    cross_send,
    cross_recv,
    group_send,
    group_recv,
    pair_send,
    pair_recv,
    end_send,
    end_recv,
    decay_send,
    decay_recv,
    carry_send,
    carry_recv,
    small_sem,
):
    blocks, count, height, width, group = dims
    cells = height * width
    rows = group * cells
    groups_n = count // group
    part = running.shape[2]
    feats = out_ref.shape[1]
    chans = 2 * part
    me = lax.axis_index("chan")
    other = 1 - me
    z = lax.axis_index("tm")
    y = lax.axis_index("groups")
    d = lax.axis_index("dp")
    quarter = frames_buf.shape[1] // 4

    def frame_copy(g):
        span = pl.ds(pl.multiple_of(g * rows, rows), rows)
        return pltpu.make_async_copy(
            frames_hbm.at[span], frames_buf.at[span], frame_sem.at[g]
        )

    def w_in_copy(tap):
        row_off, col_off = tap // 3, tap % 3
        place = (col_off * 3 + row_off) * part
        return pltpu.make_async_copy(
            w_in_hbm.at[tap], w_in_buf.at[:, place : place + part], w_in_sem.at[tap]
        )

    w_out_copy = pltpu.make_async_copy(w_out_hbm, w_out_buf, w_out_sem)
    small = [
        pltpu.make_async_copy(steps_hbm, steps_ref, small_sem.at[0]),
        pltpu.make_async_copy(rates_hbm, rates_ref, small_sem.at[1]),
        pltpu.make_async_copy(skip_hbm, skip_ref, small_sem.at[2]),
    ]
    for copy in small:
        copy.start()
    for tap in range(9):
        w_in_copy(tap).start()
    for g in range(groups_n):
        frame_copy(g).start()
    w_out_copy.start()

    barrier = pltpu.get_barrier_semaphore()
    pl.semaphore_signal(barrier, inc=1, device_id={"chan": other}, device_id_type=MESH)
    pl.semaphore_signal(barrier, inc=1, device_id={"groups": 1 - y}, device_id_type=MESH)
    pl.semaphore_signal(barrier, inc=1, device_id={"dp": 1 - d}, device_id_type=MESH)
    for k in range(blocks):

        @pl.when(k != z)
        def _():
            pl.semaphore_signal(barrier, inc=1, device_id={"tm": k}, device_id_type=MESH)

    for copy in small:
        copy.wait()
    rates_all = rates_ref[...]
    rates_own = rates_ref[:, pl.ds(pl.multiple_of(me * part, part), part)]
    rates_far = rates_ref[:, pl.ds(pl.multiple_of(other * part, part), part)]
    total = steps_ref[0, 0]
    for t in range(1, count):
        total = total + steps_ref[0, t]
    block_decay[z] = jnp.broadcast_to(jnp.exp(-rates_own * total), (8, part))
    running[...] = jnp.zeros_like(running)
    taps[...] = jnp.zeros_like(taps)
    pl.semaphore_wait(barrier, blocks + 2)

    def decay_send_to(k):
        return pltpu.make_async_remote_copy(
            src_ref=block_decay.at[z],
            dst_ref=block_decay.at[z],
            send_sem=decay_send.at[k],
            recv_sem=decay_recv.at[z],
            device_id={"tm": k},
            device_id_type=MESH,
        )

    def decay_from(k):
        return pltpu.make_async_remote_copy(
            src_ref=block_decay.at[k],
            dst_ref=block_decay.at[k],
            send_sem=decay_send.at[k],
            recv_sem=decay_recv.at[k],
            device_id={"tm": k},
            device_id_type=MESH,
        )

    def end_send_to(k):
        return pltpu.make_async_remote_copy(
            src_ref=ends.at[z],
            dst_ref=ends.at[z],
            send_sem=end_send.at[k],
            recv_sem=end_recv.at[z],
            device_id={"tm": k},
            device_id_type=MESH,
        )

    def end_from(k):
        return pltpu.make_async_remote_copy(
            src_ref=ends.at[k],
            dst_ref=ends.at[k],
            send_sem=end_send.at[k],
            recv_sem=end_recv.at[k],
            device_id={"tm": k},
            device_id_type=MESH,
        )

    def piece(buffer, row, place):
        return buffer.at[
            pl.ds(pl.multiple_of(row * quarter, quarter), quarter),
            pl.ds(pl.multiple_of(place * part, part), part),
        ]

    def cross_copy(place):
        return pltpu.make_async_remote_copy(
            src_ref=piece(w_in_buf, 2 * y + d, place),
            dst_ref=piece(w_far_buf, 2 * y + d, place),
            send_sem=cross_send.at[place],
            recv_sem=cross_recv.at[place],
            device_id={"chan": other},
            device_id_type=MESH,
        )

    def group_copy(place, row):
        return pltpu.make_async_remote_copy(
            src_ref=piece(w_far_buf, row, place),
            dst_ref=piece(w_far_buf, row, place),
            send_sem=group_send.at[place],
            recv_sem=group_recv.at[place],
            device_id={"groups": 1 - y},
            device_id_type=MESH,
        )

    def pair_copy(slot, place, row):
        return pltpu.make_async_remote_copy(
            src_ref=piece(w_far_buf, row, place),
            dst_ref=piece(w_far_buf, row, place),
            send_sem=pair_send.at[slot, place],
            recv_sem=pair_recv.at[slot, place],
            device_id={"dp": 1 - d},
            device_id_type=MESH,
        )

    near, away = 2 * y + d, 2 * (1 - y) + d
    near_pair, away_pair = 2 * y + 1 - d, 2 * (1 - y) + 1 - d

    def pass_on(place):
        cross_copy(place).wait_recv()
        group_copy(place, near).start()
        pair_copy(0, place, near).start()

    def pass_pair(place):
        group_copy(place, away).wait_recv()
        pair_copy(1, place, away).start()

    def pair_arrive(place):
        pair_copy(0, place, near_pair).wait_recv()
        pair_copy(1, place, away_pair).wait_recv()

    def carry_copy(side):
        return pltpu.make_async_remote_copy(
            src_ref=carry.at[side],
            dst_ref=carry.at[side],
            send_sem=carry_send,
            recv_sem=carry_recv,
            device_id={"chan": other},
            device_id_type=MESH,
        )

    for place in range(9):
        w_in_copy((place % 3) * 3 + place // 3).wait()
        cross_copy(place).start()
    for k in range(1, blocks):

        @pl.when(z < k)
        def _():
            decay_send_to(k).start()

    column = lax.broadcasted_iota(jnp.int32, (cells, 1), 0) % width
    first_col = column == 0
    last_col = column == width - 1

    def displaced_sum(mine, base):
        zero = jnp.zeros((width, part), jnp.float32)
        above = mine[:, base : base + part]
        level = mine[:, base + part : base + 2 * part]
        below = mine[:, base + 2 * part : base + 3 * part]
        return (
            level
            + jnp.concatenate([zero, above[: cells - width]], axis=0)
            + jnp.concatenate([below[width:], zero], axis=0)
        )

    def from_left(values):
        return jnp.where(first_col, 0.0, pltpu.roll(values, 1, 0))

    def from_right(values):
        return jnp.where(last_col, 0.0, pltpu.roll(values, cells - 1, 0))

    def advance(side, t, rates_part, drive):
        decay = jnp.exp(-(rates_part * steps_ref[0, t]))
        gain_in = (1.0 - decay) / rates_part
        state = decay * running[side] + gain_in * drive
        running[side] = state
        states[side, t] = state

    def drive_step(g, unused):
        frame_copy(g).wait()
        span = pl.ds(pl.multiple_of(g * rows, rows), rows)
        product = jnp.dot(
            frames_buf[span, :], w_in_buf[...], preferred_element_type=jnp.float32
        )
        for f in range(group):
            mine = product[f * cells : (f + 1) * cells]
            drive = (
                displaced_sum(mine, 3 * part)
                + from_left(displaced_sum(mine, 0))
                + from_right(displaced_sum(mine, 6 * part))
            )
            advance(me, g * group + f, rates_own, drive)

        @pl.when(g > 0)
        def _():
            pass_on(g - 1)

        return unused

    def far_step(col_off, g, unused):
        span = pl.ds(pl.multiple_of(g * rows, rows), rows)
        product = jnp.dot(
            frames_buf[span, :],
            w_far_buf[:, col_off * 3 * part : (col_off + 1) * 3 * part],
            preferred_element_type=jnp.float32,
        )
        for f in range(group):
            t = g * group + f
            sums = displaced_sum(product[f * cells : (f + 1) * cells], 0)
            if col_off == 0:
                far_drive[t] = from_left(sums)
            elif col_off == 1:
                far_drive[t] = far_drive[t] + sums
            else:
                advance(other, t, rates_far, far_drive[t] + from_right(sums))
        return unused

    def far_part(col_off):
        for place in range(3 * col_off, 3 * col_off + 3):
            pair_arrive(place)
        lax.fori_loop(0, groups_n, functools.partial(far_step, col_off), 0)

    lax.fori_loop(0, groups_n, drive_step, 0)
    ends[z] = running[me].astype(jnp.bfloat16)

    for k in reversed(range(1, blocks)):

        @pl.when(z < k)
        def _():
            end_send_to(k).start()

    passed = groups_n - 1
    for place in range(passed, 5):
        pass_on(place)
    for place in range(3):
        pass_pair(place)
    far_part(0)
    for place in range(5, 8):
        pass_on(place)
    for place in range(3, 6):
        pass_pair(place)
    pass_on(8)
    far_part(1)

    running[me] = jnp.zeros_like(running[me])
    for k in range(blocks - 1):

        @pl.when(k < z)
        def _():
            decay_from(k).wait_recv()
            end_from(k).wait_recv()
            running[me] = block_decay[k][:1] * running[me] + ends[k].astype(jnp.float32)

    carry[me] = running[me].astype(jnp.bfloat16)
    carry_copy(me).start()
    for place in range(6, 9):
        pass_pair(place)
    far_part(2)
    w_out_copy.wait()
    carry_copy(other).wait_recv()

    own_feats = pl.ds(pl.multiple_of(me * feats, feats), feats)

    def mix_step(g, elapsed):
        span = pl.ds(pl.multiple_of(g * rows, rows), rows)
        for f in range(group):
            t = g * group + f
            elapsed = elapsed + steps_ref[0, t]
            product = jnp.exp(-rates_all * elapsed)
            for side in range(2):
                lanes = slice(side * part, (side + 1) * part)
                state = states[side, t] + product[:, lanes] * carry[
                    side
                ].astype(jnp.float32)
                state = state.astype(jnp.bfloat16).astype(jnp.float32)
                held = (
                    jnp.where(first_col, 0.0, pltpu.roll(state, 1, 0)),
                    state,
                    jnp.where(last_col, 0.0, pltpu.roll(state, cells - 1, 0)),
                )
                for col_off in range(3):
                    at = col_off * chans + side * part
                    taps[f, width : width + cells, at : at + part] = held[col_off].astype(
                        jnp.bfloat16
                    )
        result = None
        for row_off in range(3):
            window = taps[:, row_off * width : row_off * width + cells, :].reshape(rows, 3 * chans)
            term = jnp.dot(
                window,
                w_out_buf[row_off * 3 * chans : (row_off + 1) * 3 * chans, :],
                preferred_element_type=jnp.float32,
            )
            result = term if result is None else result + term
        result = result + skip_ref[...] * frames_buf[span, own_feats].astype(jnp.float32)
        out_ref[span, :] = result.astype(jnp.bfloat16)
        return elapsed

    lax.fori_loop(0, groups_n, mix_step, jnp.float32(0.0))

    for place in range(9):
        cross_copy(place).wait_send()
        group_copy(place, near).wait_send()
        pair_copy(0, place, near).wait_send()
        pair_copy(1, place, away).wait_send()
    carry_copy(me).wait_send()
    for k in range(1, blocks):

        @pl.when(z < k)
        def _():
            decay_send_to(k).wait_send()
            end_send_to(k).wait_send()


def on_device_fused(frames, w_in, w_out, skip, rates, steps_dt):
    _, count, height, width, feats_in = frames.shape
    part, feats = w_in.shape[3], w_out.shape[3]
    chans = w_out.shape[2]
    blocks = lax.axis_size("tm")
    cells = height * width
    group = 2
    groups_n = count // group
    dims = (blocks, count, height, width, group)
    hbm = pl.BlockSpec(memory_space=pltpu.HBM)
    dma = pltpu.SemaphoreType.DMA
    out = pl.pallas_call(
        functools.partial(fused_kernel, dims),
        out_shape=jax.ShapeDtypeStruct((count * cells, feats), jnp.bfloat16),
        in_specs=[hbm] * 6,
        out_specs=pl.BlockSpec(memory_space=pltpu.VMEM),
        scratch_shapes=[
            pltpu.VMEM((1, feats), jnp.float32),
            pltpu.VMEM((1, chans), jnp.float32),
            pltpu.SMEM((1, count), jnp.float32),
            pltpu.VMEM((count * cells, feats_in), jnp.bfloat16),
            pltpu.VMEM((feats_in, 9 * part), jnp.bfloat16),
            pltpu.VMEM((feats_in, 9 * part), jnp.bfloat16),
            pltpu.VMEM((9 * chans, feats), jnp.bfloat16),
            pltpu.VMEM((2, count, cells, part), jnp.float32),
            pltpu.VMEM((2, cells, part), jnp.float32),
            pltpu.VMEM((count, cells, part), jnp.float32),
            pltpu.VMEM((blocks, cells, part), jnp.bfloat16),
            pltpu.VMEM((blocks, 8, part), jnp.float32),
            pltpu.VMEM((2, cells, part), jnp.bfloat16),
            pltpu.VMEM((group, cells + 2 * width, 3 * chans), jnp.bfloat16),
            dma((groups_n,)),
            dma((9,)),
            dma,
            dma((9,)),
            dma((9,)),
            dma((9,)),
            dma((9,)),
            dma((2, 9)),
            dma((2, 9)),
            dma((blocks,)),
            dma((blocks,)),
            dma((blocks,)),
            dma((blocks,)),
            dma,
            dma,
            dma((3,)),
        ],
        compiler_params=pltpu.CompilerParams(
            collective_id=0, has_side_effects=True, vmem_limit_bytes=62 << 20
        ),
    )(
        frames.reshape(count * cells, feats_in),
        w_in.reshape(9, feats_in, part),
        w_out.reshape(9 * chans, feats),
        skip.reshape(1, feats),
        rates.reshape(1, chans),
        steps_dt,
    )
    return out.reshape(1, count, height, width, feats)


def pick(mesh, frames, w_in, w_out, skip, rates, steps_dt):
    clips, count, height, width = frames.shape[:4]
    fused = (
        mesh.shape["chan"] == 2
        and mesh.shape["groups"] == 2
        and mesh.shape["dp"] == 2
        and clips == 1
        and count == 8
        and width == 16
        and w_in.shape[3] == LANES
        and w_out.shape[3] % LANES == 0
    )
    body = on_device_fused if fused else on_device
    return body(frames, w_in, w_out, skip, rates, steps_dt)


def solution(mesh):
    return jax.shard_map(
        functools.partial(pick, mesh),
        mesh=mesh,
        in_specs=(
            P(("groups", "dp"), "tm", None, None, None),
            P(None, None, None, "chan"),
            P(None, None, None, "chan"),
            P("chan"),
            P(),
            P(("groups", "dp"), "tm"),
        ),
        out_specs=P(("groups", "dp"), "tm", None, None, "chan"),
        check_vma=False,
    )
```

```python
import functools

import jax
import jax.numpy as jnp
from jax import lax
from jax.experimental import pallas as pl
from jax.experimental.pallas import tpu as pltpu
from jax.sharding import PartitionSpec as P


def from_behind(block, axis, distance):
    devices = range(lax.axis_size(axis))
    route = [(i - distance, i) for i in devices if i - distance in devices]
    return lax.ppermute(block, axis, route)


def pad_grid(values):
    return jnp.pad(values, ((0, 0), (0, 0), (1, 1), (1, 1), (0, 0)))


def displaced_filter(padded, weight, total):
    height = padded.shape[2] - 2
    width = padded.shape[3] - 2
    channels = padded.shape[4]
    for row_off in range(3):
        for col_off in range(3):
            window = padded[:, :, row_off : row_off + height, col_off : col_off + width, :].reshape(
                -1, channels
            )
            term = jnp.dot(window, weight[row_off, col_off], preferred_element_type=jnp.float32)
            total = total + term.reshape(total.shape)
    return total


def combine_operator(earlier, later):
    return (earlier[0] * later[0], later[0] * earlier[1] + later[1])


def block_states(frames, weight_in, rate_part, steps_dt):
    batch_n, frame_n, height, width = frames.shape[:4]
    chans = weight_in.shape[3]
    shape_out = frames.shape[:4] + (chans,)
    drive = displaced_filter(pad_grid(frames), weight_in, jnp.zeros(shape_out, jnp.float32))
    flat_drive = drive.reshape(batch_n, frame_n, height, width * chans)
    scaled = rate_part[None, None, :] * steps_dt[:, :, None]
    decay = jnp.exp(-scaled)
    gain_in = -jnp.expm1(-scaled) / rate_part[None, None, :]
    decay_flat = jnp.tile(decay, (1, 1, width))[:, :, None, :]
    gain_flat = jnp.tile(gain_in, (1, 1, width))[:, :, None, :]
    running_product, local_state = lax.associative_scan(
        combine_operator, (decay_flat, gain_flat * flat_drive), axis=1
    )
    total_decay = running_product[:, -1]
    end_state = local_state[:, -1]

    def relay(index, incoming):
        return from_behind(total_decay * incoming + end_state, "tm", 1)

    carried = lax.fori_loop(0, lax.axis_size("tm") - 1, relay, jnp.zeros_like(end_state))
    full_state = local_state + running_product * carried[:, None]
    return full_state.astype(jnp.bfloat16)


def on_device(frames, w_in, w_out, skip, rates, steps_dt):
    feat_part = w_out.shape[3]
    state_part = w_in.shape[3]
    batch_n, frame_n, height, width = frames.shape[:4]
    own_chan = lax.axis_index("chan")
    out_shape = frames.shape[:4] + (feat_part,)
    rate_part = lax.dynamic_slice_in_dim(rates, own_chan * state_part, state_part, 0)
    flat_states = block_states(frames, w_in, rate_part, steps_dt)
    block_width = width * state_part
    piece = lax.all_gather(flat_states, "chan", axis=3, tiled=True)
    partitions = piece.shape[3] // block_width
    grid = piece.reshape(batch_n, frame_n, height, partitions, width, state_part)
    grid = jnp.moveaxis(grid, 3, 4).reshape(
        batch_n, frame_n, height, width, partitions * state_part
    )
    outcome = displaced_filter(pad_grid(grid), w_out, jnp.zeros(out_shape, jnp.float32))
    own_feats = lax.dynamic_slice_in_dim(frames, own_chan * feat_part, feat_part, 4)
    mixed = outcome + skip * own_feats.astype(jnp.float32)
    return mixed.astype(jnp.bfloat16)


LANES = 128
MESH = pl.DeviceIdType.MESH


def fused_kernel(
    dims,
    frames_hbm,
    w_in_hbm,
    w_out_hbm,
    skip_hbm,
    rates_hbm,
    steps_hbm,
    out_hbm,
    skip_ref,
    rates_ref,
    steps_ref,
    frames_buf,
    w_in_buf,
    w_out_buf,
    out_buf,
    states,
    running,
    ends,
    block_decay,
    carry,
    taps,
    frame_sem,
    w_in_sem,
    w_out_sem,
    out_sem,
    state_send,
    state_recv,
    end_send,
    end_recv,
    decay_send,
    decay_recv,
    carry_send,
    carry_recv,
    small_sem,
):
    blocks, count, height, width, group = dims
    cells = height * width
    rows = group * cells
    groups_n = count // group
    early = (5 * count) // 8
    part = running.shape[1]
    feats = out_buf.shape[1]
    chans = 2 * part
    me = lax.axis_index("chan")
    other = 1 - me
    z = lax.axis_index("tm")

    def frame_copy(g):
        span = pl.ds(pl.multiple_of(g * rows, rows), rows)
        return pltpu.make_async_copy(
            frames_hbm.at[span], frames_buf.at[span], frame_sem.at[g]
        )

    def w_in_copy(tap):
        row_off, col_off = tap // 3, tap % 3
        place = (col_off * 3 + row_off) * part
        return pltpu.make_async_copy(
            w_in_hbm.at[tap], w_in_buf.at[:, place : place + part], w_in_sem.at[tap]
        )

    def out_copy(g):
        span = pl.ds(pl.multiple_of(g * rows, rows), rows)
        return pltpu.make_async_copy(out_buf.at[span], out_hbm.at[span], out_sem.at[g])

    w_out_copy = pltpu.make_async_copy(w_out_hbm, w_out_buf, w_out_sem)
    small = [
        pltpu.make_async_copy(steps_hbm, steps_ref, small_sem.at[0]),
        pltpu.make_async_copy(rates_hbm, rates_ref, small_sem.at[1]),
        pltpu.make_async_copy(skip_hbm, skip_ref, small_sem.at[2]),
    ]
    for copy in small:
        copy.start()
    for tap in range(9):
        w_in_copy(tap).start()
    for g in range(groups_n):
        frame_copy(g).start()
    w_out_copy.start()

    barrier = pltpu.get_barrier_semaphore()
    pl.semaphore_signal(barrier, inc=1, device_id={"chan": other}, device_id_type=MESH)
    for k in range(blocks):

        @pl.when(k != z)
        def _():
            pl.semaphore_signal(barrier, inc=1, device_id={"tm": k}, device_id_type=MESH)

    for copy in small:
        copy.wait()
    rates_all = rates_ref[...]
    rates_own = rates_ref[:, pl.ds(pl.multiple_of(me * part, part), part)]
    total = steps_ref[0, 0]
    for t in range(1, count):
        total = total + steps_ref[0, t]
    block_decay[z] = jnp.broadcast_to(jnp.exp(-rates_own * total), (8, part))
    running[...] = jnp.zeros_like(running)
    taps[...] = jnp.zeros_like(taps)
    pl.semaphore_wait(barrier, blocks)

    def decay_send_to(k):
        return pltpu.make_async_remote_copy(
            src_ref=block_decay.at[z],
            dst_ref=block_decay.at[z],
            send_sem=decay_send.at[k],
            recv_sem=decay_recv.at[z],
            device_id={"tm": k},
            device_id_type=MESH,
        )

    def decay_from(k):
        return pltpu.make_async_remote_copy(
            src_ref=block_decay.at[k],
            dst_ref=block_decay.at[k],
            send_sem=decay_send.at[k],
            recv_sem=decay_recv.at[k],
            device_id={"tm": k},
            device_id_type=MESH,
        )

    def end_send_to(k):
        return pltpu.make_async_remote_copy(
            src_ref=states.at[me, count - 1],
            dst_ref=ends.at[z],
            send_sem=end_send.at[k],
            recv_sem=end_recv.at[z],
            device_id={"tm": k},
            device_id_type=MESH,
        )

    def end_from(k):
        return pltpu.make_async_remote_copy(
            src_ref=states.at[me, count - 1],
            dst_ref=ends.at[k],
            send_sem=end_send.at[k],
            recv_sem=end_recv.at[k],
            device_id={"tm": k},
            device_id_type=MESH,
        )

    def state_copy(side, t):
        return pltpu.make_async_remote_copy(
            src_ref=states.at[side, t],
            dst_ref=states.at[side, t],
            send_sem=state_send.at[t],
            recv_sem=state_recv.at[t],
            device_id={"chan": other},
            device_id_type=MESH,
        )

    def carry_copy(side):
        return pltpu.make_async_remote_copy(
            src_ref=carry.at[side],
            dst_ref=carry.at[side],
            send_sem=carry_send,
            recv_sem=carry_recv,
            device_id={"chan": other},
            device_id_type=MESH,
        )

    for k in range(1, blocks):

        @pl.when(z < k)
        def _():
            decay_send_to(k).start()

    for tap in range(9):
        w_in_copy(tap).wait()

    column = lax.broadcasted_iota(jnp.int32, (cells, 1), 0) % width
    first_col = column == 0
    last_col = column == width - 1

    def drive_step(g, unused):
        frame_copy(g).wait()
        span = pl.ds(pl.multiple_of(g * rows, rows), rows)
        product = jnp.dot(
            frames_buf[span, :], w_in_buf[...], preferred_element_type=jnp.float32
        )
        for f in range(group):
            t = g * group + f
            mine = product[f * cells : (f + 1) * cells]
            sums = []
            for col_off in range(3):
                base = col_off * 3 * part
                above = mine[:, base : base + part]
                level = mine[:, base + part : base + 2 * part]
                below = mine[:, base + 2 * part : base + 3 * part]
                zero = jnp.zeros((width, part), jnp.float32)
                sums.append(
                    level
                    + jnp.concatenate([zero, above[: cells - width]], axis=0)
                    + jnp.concatenate([below[width:], zero], axis=0)
                )
            drive = (
                sums[1]
                + jnp.where(first_col, 0.0, pltpu.roll(sums[0], 1, 0))
                + jnp.where(last_col, 0.0, pltpu.roll(sums[2], cells - 1, 0))
            )
            scaled = rates_own * steps_ref[0, t]
            decay = jnp.exp(-scaled)
            gain_in = (1.0 - decay) / rates_own
            state = decay * running[...] + gain_in * drive
            running[...] = state
            states[me, t] = state.astype(jnp.bfloat16)

            @pl.when(t < early)
            def _():
                state_copy(me, t).start()

        return unused

    lax.fori_loop(0, groups_n, drive_step, 0)

    for k in reversed(range(1, blocks)):

        @pl.when(z < k)
        def _():
            end_send_to(k).start()

    running[...] = jnp.zeros_like(running)
    for k in range(blocks - 1):

        @pl.when(k < z)
        def _():
            decay_from(k).wait_recv()
            end_from(k).wait_recv()
            running[...] = block_decay[k][:1] * running[...] + ends[k].astype(jnp.float32)

    carry[me] = running[...].astype(jnp.bfloat16)
    carry_copy(me).start()
    for t in range(early, count):
        state_copy(me, t).start()
    w_out_copy.wait()
    carry_copy(other).wait_recv()

    own_feats = pl.ds(pl.multiple_of(me * feats, feats), feats)

    def mix_step(g, elapsed):
        span = pl.ds(pl.multiple_of(g * rows, rows), rows)
        for f in range(group):
            t = g * group + f
            state_copy(other, t).wait_recv()
            elapsed = elapsed + steps_ref[0, t]
            product = jnp.exp(-rates_all * elapsed)
            for side in range(2):
                lanes = slice(side * part, (side + 1) * part)
                state = states[side, t].astype(jnp.float32) + product[:, lanes] * carry[
                    side
                ].astype(jnp.float32)
                state = state.astype(jnp.bfloat16).astype(jnp.float32)
                held = (
                    jnp.where(first_col, 0.0, pltpu.roll(state, 1, 0)),
                    state,
                    jnp.where(last_col, 0.0, pltpu.roll(state, cells - 1, 0)),
                )
                for col_off in range(3):
                    at = col_off * chans + side * part
                    taps[f, width : width + cells, at : at + part] = held[col_off].astype(
                        jnp.bfloat16
                    )
        result = None
        for row_off in range(3):
            window = taps[:, row_off * width : row_off * width + cells, :].reshape(rows, 3 * chans)
            term = jnp.dot(
                window,
                w_out_buf[row_off * 3 * chans : (row_off + 1) * 3 * chans, :],
                preferred_element_type=jnp.float32,
            )
            result = term if result is None else result + term
        result = result + skip_ref[...] * frames_buf[span, own_feats].astype(jnp.float32)
        out_buf[span, :] = result.astype(jnp.bfloat16)
        out_copy(g).start()
        return elapsed

    lax.fori_loop(0, groups_n, mix_step, jnp.float32(0.0))

    for g in range(groups_n):
        out_copy(g).wait()
    for t in range(count):
        state_copy(me, t).wait_send()
    carry_copy(me).wait_send()
    for k in range(1, blocks):

        @pl.when(z < k)
        def _():
            decay_send_to(k).wait_send()
            end_send_to(k).wait_send()


def on_device_fused(frames, w_in, w_out, skip, rates, steps_dt):
    _, count, height, width, feats_in = frames.shape
    part, feats = w_in.shape[3], w_out.shape[3]
    chans = w_out.shape[2]
    blocks = lax.axis_size("tm")
    cells = height * width
    group = 2
    groups_n = count // group
    dims = (blocks, count, height, width, group)
    hbm = pl.BlockSpec(memory_space=pltpu.HBM)
    dma = pltpu.SemaphoreType.DMA
    out = pl.pallas_call(
        functools.partial(fused_kernel, dims),
        out_shape=jax.ShapeDtypeStruct((count * cells, feats), jnp.bfloat16),
        in_specs=[hbm] * 6,
        out_specs=pl.BlockSpec(memory_space=pl.ANY),
        scratch_shapes=[
            pltpu.VMEM((1, feats), jnp.float32),
            pltpu.VMEM((1, chans), jnp.float32),
            pltpu.SMEM((1, count), jnp.float32),
            pltpu.VMEM((count * cells, feats_in), jnp.bfloat16),
            pltpu.VMEM((feats_in, 9 * part), jnp.bfloat16),
            pltpu.VMEM((9 * chans, feats), jnp.bfloat16),
            pltpu.VMEM((count * cells, feats), jnp.bfloat16),
            pltpu.VMEM((2, count, cells, part), jnp.bfloat16),
            pltpu.VMEM((cells, part), jnp.float32),
            pltpu.VMEM((blocks, cells, part), jnp.bfloat16),
            pltpu.VMEM((blocks, 8, part), jnp.float32),
            pltpu.VMEM((2, cells, part), jnp.bfloat16),
            pltpu.VMEM((group, cells + 2 * width, 3 * chans), jnp.bfloat16),
            dma((groups_n,)),
            dma((9,)),
            dma,
            dma((groups_n,)),
            dma((count,)),
            dma((count,)),
            dma((blocks,)),
            dma((blocks,)),
            dma((blocks,)),
            dma((blocks,)),
            dma,
            dma,
            dma((3,)),
        ],
        compiler_params=pltpu.CompilerParams(
            collective_id=0, has_side_effects=True, vmem_limit_bytes=62 << 20
        ),
    )(
        frames.reshape(count * cells, feats_in),
        w_in.reshape(9, feats_in, part),
        w_out.reshape(9 * chans, feats),
        skip.reshape(1, feats),
        rates.reshape(1, chans),
        steps_dt,
    )
    return out.reshape(1, count, height, width, feats)


def pick(mesh, frames, w_in, w_out, skip, rates, steps_dt):
    clips, count, height, width = frames.shape[:4]
    fused = (
        mesh.shape["chan"] == 2
        and clips == 1
        and count % 2 == 0
        and width == 16
        and w_in.shape[3] == LANES
        and w_out.shape[3] % LANES == 0
    )
    body = on_device_fused if fused else on_device
    return body(frames, w_in, w_out, skip, rates, steps_dt)


def solution(mesh):
    return jax.shard_map(
        functools.partial(pick, mesh),
        mesh=mesh,
        in_specs=(
            P(("groups", "dp"), "tm", None, None, None),
            P(None, None, None, "chan"),
            P(None, None, None, "chan"),
            P("chan"),
            P(),
            P(("groups", "dp"), "tm"),
        ),
        out_specs=P(("groups", "dp"), "tm", None, None, "chan"),
        check_vma=False,
    )
```

```python
import functools

import jax
import jax.numpy as jnp
from jax import lax
from jax.experimental import pallas as pl
from jax.experimental.pallas import tpu as pltpu
from jax.sharding import PartitionSpec as P


def from_behind(block, axis, distance):
    devices = range(lax.axis_size(axis))
    route = [(i - distance, i) for i in devices if i - distance in devices]
    return lax.ppermute(block, axis, route)


def pad_grid(values):
    return jnp.pad(values, ((0, 0), (0, 0), (1, 1), (1, 1), (0, 0)))


def displaced_filter(padded, weight, total):
    height = padded.shape[2] - 2
    width = padded.shape[3] - 2
    channels = padded.shape[4]
    for row_off in range(3):
        for col_off in range(3):
            window = padded[:, :, row_off : row_off + height, col_off : col_off + width, :].reshape(
                -1, channels
            )
            term = jnp.dot(window, weight[row_off, col_off], preferred_element_type=jnp.float32)
            total = total + term.reshape(total.shape)
    return total


def combine_operator(earlier, later):
    return (earlier[0] * later[0], later[0] * earlier[1] + later[1])


def block_states(frames, weight_in, rate_part, steps_dt):
    batch_n, frame_n, height, width = frames.shape[:4]
    chans = weight_in.shape[3]
    shape_out = frames.shape[:4] + (chans,)
    drive = displaced_filter(pad_grid(frames), weight_in, jnp.zeros(shape_out, jnp.float32))
    flat_drive = drive.reshape(batch_n, frame_n, height, width * chans)
    scaled = rate_part[None, None, :] * steps_dt[:, :, None]
    decay = jnp.exp(-scaled)
    gain_in = -jnp.expm1(-scaled) / rate_part[None, None, :]
    decay_flat = jnp.tile(decay, (1, 1, width))[:, :, None, :]
    gain_flat = jnp.tile(gain_in, (1, 1, width))[:, :, None, :]
    running_product, local_state = lax.associative_scan(
        combine_operator, (decay_flat, gain_flat * flat_drive), axis=1
    )
    total_decay = running_product[:, -1]
    end_state = local_state[:, -1]

    def relay(index, incoming):
        return from_behind(total_decay * incoming + end_state, "tm", 1)

    carried = lax.fori_loop(0, lax.axis_size("tm") - 1, relay, jnp.zeros_like(end_state))
    full_state = local_state + running_product * carried[:, None]
    return full_state.astype(jnp.bfloat16)


def on_device(frames, w_in, w_out, skip, rates, steps_dt):
    feat_part = w_out.shape[3]
    state_part = w_in.shape[3]
    batch_n, frame_n, height, width = frames.shape[:4]
    own_chan = lax.axis_index("chan")
    out_shape = frames.shape[:4] + (feat_part,)
    rate_part = lax.dynamic_slice_in_dim(rates, own_chan * state_part, state_part, 0)
    flat_states = block_states(frames, w_in, rate_part, steps_dt)
    block_width = width * state_part
    piece = lax.all_gather(flat_states, "chan", axis=3, tiled=True)
    partitions = piece.shape[3] // block_width
    grid = piece.reshape(batch_n, frame_n, height, partitions, width, state_part)
    grid = jnp.moveaxis(grid, 3, 4).reshape(
        batch_n, frame_n, height, width, partitions * state_part
    )
    outcome = displaced_filter(pad_grid(grid), w_out, jnp.zeros(out_shape, jnp.float32))
    own_feats = lax.dynamic_slice_in_dim(frames, own_chan * feat_part, feat_part, 4)
    mixed = outcome + skip * own_feats.astype(jnp.float32)
    return mixed.astype(jnp.bfloat16)


LANES = 128
MESH = pl.DeviceIdType.MESH


def fused_kernel(
    dims,
    frames_hbm,
    w_in_hbm,
    w_out_hbm,
    skip_hbm,
    rates_hbm,
    steps_hbm,
    out_ref,
    skip_ref,
    rates_ref,
    steps_ref,
    frames_buf,
    w_in_buf,
    w_out_buf,
    states,
    running,
    ends,
    block_decay,
    carry,
    taps,
    frame_sem,
    w_in_sem,
    w_out_sem,
    state_send,
    state_recv,
    end_send,
    end_recv,
    decay_send,
    decay_recv,
    carry_send,
    carry_recv,
    small_sem,
):
    blocks, count, height, width, group = dims
    cells = height * width
    rows = group * cells
    groups_n = count // group
    early = (5 * count) // 8
    part = running.shape[1]
    feats = out_ref.shape[1]
    chans = 2 * part
    me = lax.axis_index("chan")
    other = 1 - me
    z = lax.axis_index("tm")

    def frame_copy(g):
        span = pl.ds(pl.multiple_of(g * rows, rows), rows)
        return pltpu.make_async_copy(
            frames_hbm.at[span], frames_buf.at[span], frame_sem.at[g]
        )

    def w_in_copy(tap):
        row_off, col_off = tap // 3, tap % 3
        place = (col_off * 3 + row_off) * part
        return pltpu.make_async_copy(
            w_in_hbm.at[tap], w_in_buf.at[:, place : place + part], w_in_sem.at[tap]
        )

    w_out_copy = pltpu.make_async_copy(w_out_hbm, w_out_buf, w_out_sem)
    small = [
        pltpu.make_async_copy(steps_hbm, steps_ref, small_sem.at[0]),
        pltpu.make_async_copy(rates_hbm, rates_ref, small_sem.at[1]),
        pltpu.make_async_copy(skip_hbm, skip_ref, small_sem.at[2]),
    ]
    for copy in small:
        copy.start()
    for tap in range(9):
        w_in_copy(tap).start()
    for g in range(groups_n):
        frame_copy(g).start()
    w_out_copy.start()

    barrier = pltpu.get_barrier_semaphore()
    pl.semaphore_signal(barrier, inc=1, device_id={"chan": other}, device_id_type=MESH)
    for k in range(blocks):

        @pl.when(k != z)
        def _():
            pl.semaphore_signal(barrier, inc=1, device_id={"tm": k}, device_id_type=MESH)

    for copy in small:
        copy.wait()
    rates_all = rates_ref[...]
    rates_own = rates_ref[:, pl.ds(pl.multiple_of(me * part, part), part)]
    total = steps_ref[0, 0]
    for t in range(1, count):
        total = total + steps_ref[0, t]
    block_decay[z] = jnp.broadcast_to(jnp.exp(-rates_own * total), (8, part))
    running[...] = jnp.zeros_like(running)
    taps[...] = jnp.zeros_like(taps)
    pl.semaphore_wait(barrier, blocks)

    def decay_send_to(k):
        return pltpu.make_async_remote_copy(
            src_ref=block_decay.at[z],
            dst_ref=block_decay.at[z],
            send_sem=decay_send.at[k],
            recv_sem=decay_recv.at[z],
            device_id={"tm": k},
            device_id_type=MESH,
        )

    def decay_from(k):
        return pltpu.make_async_remote_copy(
            src_ref=block_decay.at[k],
            dst_ref=block_decay.at[k],
            send_sem=decay_send.at[k],
            recv_sem=decay_recv.at[k],
            device_id={"tm": k},
            device_id_type=MESH,
        )

    def end_send_to(k):
        return pltpu.make_async_remote_copy(
            src_ref=states.at[me, count - 1],
            dst_ref=ends.at[z],
            send_sem=end_send.at[k],
            recv_sem=end_recv.at[z],
            device_id={"tm": k},
            device_id_type=MESH,
        )

    def end_from(k):
        return pltpu.make_async_remote_copy(
            src_ref=states.at[me, count - 1],
            dst_ref=ends.at[k],
            send_sem=end_send.at[k],
            recv_sem=end_recv.at[k],
            device_id={"tm": k},
            device_id_type=MESH,
        )

    def state_copy(side, t):
        return pltpu.make_async_remote_copy(
            src_ref=states.at[side, t],
            dst_ref=states.at[side, t],
            send_sem=state_send.at[t],
            recv_sem=state_recv.at[t],
            device_id={"chan": other},
            device_id_type=MESH,
        )

    def carry_copy(side):
        return pltpu.make_async_remote_copy(
            src_ref=carry.at[side],
            dst_ref=carry.at[side],
            send_sem=carry_send,
            recv_sem=carry_recv,
            device_id={"chan": other},
            device_id_type=MESH,
        )

    for k in range(1, blocks):

        @pl.when(z < k)
        def _():
            decay_send_to(k).start()

    for tap in range(9):
        w_in_copy(tap).wait()

    column = lax.broadcasted_iota(jnp.int32, (cells, 1), 0) % width
    first_col = column == 0
    last_col = column == width - 1

    def drive_step(g, unused):
        frame_copy(g).wait()
        span = pl.ds(pl.multiple_of(g * rows, rows), rows)
        product = jnp.dot(
            frames_buf[span, :], w_in_buf[...], preferred_element_type=jnp.float32
        )
        for f in range(group):
            t = g * group + f
            mine = product[f * cells : (f + 1) * cells]
            sums = []
            for col_off in range(3):
                base = col_off * 3 * part
                above = mine[:, base : base + part]
                level = mine[:, base + part : base + 2 * part]
                below = mine[:, base + 2 * part : base + 3 * part]
                zero = jnp.zeros((width, part), jnp.float32)
                sums.append(
                    level
                    + jnp.concatenate([zero, above[: cells - width]], axis=0)
                    + jnp.concatenate([below[width:], zero], axis=0)
                )
            drive = (
                sums[1]
                + jnp.where(first_col, 0.0, pltpu.roll(sums[0], 1, 0))
                + jnp.where(last_col, 0.0, pltpu.roll(sums[2], cells - 1, 0))
            )
            scaled = rates_own * steps_ref[0, t]
            decay = jnp.exp(-scaled)
            gain_in = (1.0 - decay) / rates_own
            state = decay * running[...] + gain_in * drive
            running[...] = state
            states[me, t] = state.astype(jnp.bfloat16)

            @pl.when(t < early)
            def _():
                state_copy(me, t).start()

        return unused

    lax.fori_loop(0, groups_n, drive_step, 0)

    for k in reversed(range(1, blocks)):

        @pl.when(z < k)
        def _():
            end_send_to(k).start()

    running[...] = jnp.zeros_like(running)
    for k in range(blocks - 1):

        @pl.when(k < z)
        def _():
            decay_from(k).wait_recv()
            end_from(k).wait_recv()
            running[...] = block_decay[k][:1] * running[...] + ends[k].astype(jnp.float32)

    carry[me] = running[...].astype(jnp.bfloat16)
    carry_copy(me).start()
    for t in range(early, count):
        state_copy(me, t).start()
    w_out_copy.wait()
    carry_copy(other).wait_recv()

    own_feats = pl.ds(pl.multiple_of(me * feats, feats), feats)

    def mix_step(g, elapsed):
        span = pl.ds(pl.multiple_of(g * rows, rows), rows)
        for f in range(group):
            t = g * group + f
            state_copy(other, t).wait_recv()
            elapsed = elapsed + steps_ref[0, t]
            product = jnp.exp(-rates_all * elapsed)
            for side in range(2):
                lanes = slice(side * part, (side + 1) * part)
                state = states[side, t].astype(jnp.float32) + product[:, lanes] * carry[
                    side
                ].astype(jnp.float32)
                state = state.astype(jnp.bfloat16).astype(jnp.float32)
                held = (
                    jnp.where(first_col, 0.0, pltpu.roll(state, 1, 0)),
                    state,
                    jnp.where(last_col, 0.0, pltpu.roll(state, cells - 1, 0)),
                )
                for col_off in range(3):
                    at = col_off * chans + side * part
                    taps[f, width : width + cells, at : at + part] = held[col_off].astype(
                        jnp.bfloat16
                    )
        result = None
        for row_off in range(3):
            window = taps[:, row_off * width : row_off * width + cells, :].reshape(rows, 3 * chans)
            term = jnp.dot(
                window,
                w_out_buf[row_off * 3 * chans : (row_off + 1) * 3 * chans, :],
                preferred_element_type=jnp.float32,
            )
            result = term if result is None else result + term
        result = result + skip_ref[...] * frames_buf[span, own_feats].astype(jnp.float32)
        out_ref[span, :] = result.astype(jnp.bfloat16)
        return elapsed

    lax.fori_loop(0, groups_n, mix_step, jnp.float32(0.0))

    for t in range(count):
        state_copy(me, t).wait_send()
    carry_copy(me).wait_send()
    for k in range(1, blocks):

        @pl.when(z < k)
        def _():
            decay_send_to(k).wait_send()
            end_send_to(k).wait_send()


def on_device_fused(frames, w_in, w_out, skip, rates, steps_dt):
    _, count, height, width, feats_in = frames.shape
    part, feats = w_in.shape[3], w_out.shape[3]
    chans = w_out.shape[2]
    blocks = lax.axis_size("tm")
    cells = height * width
    group = 2
    groups_n = count // group
    dims = (blocks, count, height, width, group)
    hbm = pl.BlockSpec(memory_space=pltpu.HBM)
    dma = pltpu.SemaphoreType.DMA
    out = pl.pallas_call(
        functools.partial(fused_kernel, dims),
        out_shape=jax.ShapeDtypeStruct((count * cells, feats), jnp.bfloat16),
        in_specs=[hbm] * 6,
        out_specs=pl.BlockSpec(memory_space=pltpu.VMEM),
        scratch_shapes=[
            pltpu.VMEM((1, feats), jnp.float32),
            pltpu.VMEM((1, chans), jnp.float32),
            pltpu.SMEM((1, count), jnp.float32),
            pltpu.VMEM((count * cells, feats_in), jnp.bfloat16),
            pltpu.VMEM((feats_in, 9 * part), jnp.bfloat16),
            pltpu.VMEM((9 * chans, feats), jnp.bfloat16),
            pltpu.VMEM((2, count, cells, part), jnp.bfloat16),
            pltpu.VMEM((cells, part), jnp.float32),
            pltpu.VMEM((blocks, cells, part), jnp.bfloat16),
            pltpu.VMEM((blocks, 8, part), jnp.float32),
            pltpu.VMEM((2, cells, part), jnp.bfloat16),
            pltpu.VMEM((group, cells + 2 * width, 3 * chans), jnp.bfloat16),
            dma((groups_n,)),
            dma((9,)),
            dma,
            dma((count,)),
            dma((count,)),
            dma((blocks,)),
            dma((blocks,)),
            dma((blocks,)),
            dma((blocks,)),
            dma,
            dma,
            dma((3,)),
        ],
        compiler_params=pltpu.CompilerParams(
            collective_id=0, has_side_effects=True, vmem_limit_bytes=48 << 20
        ),
    )(
        *[
            pltpu.with_memory_space_constraint(array, pltpu.HBM)
            for array in (
                frames.reshape(count * cells, feats_in),
                w_in.reshape(9, feats_in, part),
                w_out.reshape(9 * chans, feats),
                skip.reshape(1, feats),
                rates.reshape(1, chans),
                steps_dt,
            )
        ]
    )
    return out.reshape(1, count, height, width, feats)


def pick(mesh, frames, w_in, w_out, skip, rates, steps_dt):
    clips, count, height, width = frames.shape[:4]
    fused = (
        mesh.shape["chan"] == 2
        and clips == 1
        and count % 2 == 0
        and width == 16
        and w_in.shape[3] == LANES
        and w_out.shape[3] % LANES == 0
    )
    body = on_device_fused if fused else on_device
    return body(frames, w_in, w_out, skip, rates, steps_dt)


def solution(mesh):
    return jax.shard_map(
        functools.partial(pick, mesh),
        mesh=mesh,
        in_specs=(
            P(("groups", "dp"), "tm", None, None, None),
            P(None, None, None, "chan"),
            P(None, None, None, "chan"),
            P("chan"),
            P(),
            P(("groups", "dp"), "tm"),
        ),
        out_specs=P(("groups", "dp"), "tm", None, None, "chan"),
        check_vma=False,
    )
```
